512 devices in a mesh: dp: 8 (over z), space: 64 (over y, x, core).
Axes of the slice: x: 4, y: 8, z: 8, core: 2. Of those that a mesh axis runs over, the one named last changes fastest.
Arguments:
- mesh_latent: bfloat16 [8, 8192, 512], P('dp', 'space'), may hold values from -6 to 6
- grid_latent: bfloat16 [8, 32768, 512], P('dp', 'space'), may hold values from -6 to 6
- cotangent: bfloat16 [8, 32768, 512], P('dp', 'space'), may hold values from -6 to 6
- sender_slot: int32 [98304], P('space'), may hold values from 0 to 191, as said below
- send_rows: int32 [64, 4, 16], P('space'), may hold values from 0 to 127, as said below
- w_send: bfloat16 [512, 512], replicated, may hold values from -0.25 to 0.25
- w_recv: bfloat16 [512, 512], replicated, may hold values from -0.25 to 0.25
- w_node: bfloat16 [512, 512], replicated, may hold values from -0.25 to 0.25
- edge_bias: float32 [512], replicated, may hold values from -3 to 3
Outputs:
- grad_mesh: float32 [8, 8192, 512], P('dp', 'space')
- grad_grid: bfloat16 [8, 32768, 512], P('dp', 'space')
- grad_w_send: bfloat16 [512, 512], replicated
- grad_w_recv: bfloat16 [512, 512], replicated
- grad_w_node: bfloat16 [512, 512], replicated
- grad_bias: float32 [512], replicated
The draws below stay inside these ranges and needn't reach their ends.
Inputs may be any that keep to these rules, and one draw needn't show every extreme that they name: `sender_slot`: on partition p, a value v >= 128 with h = v - 128 names a halo position i = h % 16 that is filled by partition q of the steps; positions of one neighbour block that no edge names may exist. `send_rows`: within one partition and one neighbour block the rows are distinct.
All inputs are finite; a program needn't handle non-finite values.
Results may differ from the reference program's by a relative error of at most 0.012.
Values may be sent and summed in bfloat16 or wider, within the bound.
No kernel may reach another device: no remote copies, remote signals or barrier semaphores. Data moves between devices by JAX's collectives and lax.ppermute only.
A program may use at most 64 MiB of HBM per device.

```python
import jax
import jax.numpy as jnp
from jax import lax

D = 512
PIECES = 64
STRIDE = 8
M_DEV = 128
HALO = 16
EDGES_DEV = 1536
G_ROWS = 32768
M_ROWS = 8192
EDGES = 98304
DATES = 8


def halo_counts(key):
    count_key, pick_key = jax.random.split(key)
    counts = jax.random.randint(count_key, (PIECES, 4), 1, HALO + 1)
    chosen = jax.random.randint(pick_key, (4,), 0, PIECES)
    filled = jnp.arange(PIECES)[:, None] == chosen[None, :]
    return jnp.where(filled, HALO, counts).astype(jnp.int32)


def draw_send_rows(key, part):
    key = jax.random.fold_in(key, 11)
    block_keys = jax.random.split(key, PIECES * 4)
    picked = jax.vmap(lambda single: jax.random.permutation(single, M_DEV)[:HALO])(block_keys)
    return picked.reshape(PIECES, 4, HALO).astype(jnp.int32)


def draw_sender_slot(key, part):
    counts = halo_counts(key)
    key = jax.random.fold_in(key, 23)
    offset_table = jnp.array([1, -1, STRIDE, PIECES // 2], jnp.int32)
    devices = jnp.arange(PIECES, dtype=jnp.int32)[:, None]
    sources = (devices - offset_table[None, :]) % PIECES
    usable = counts[sources, jnp.arange(4)[None, :]]
    first_key, flag_key, block_key, index_key, local_key, order_key = jax.random.split(key, 6)
    lead_within = jnp.tile(jnp.arange(HALO, dtype=jnp.int32), 4)
    lead_block = jnp.repeat(jnp.arange(4, dtype=jnp.int32), HALO)
    lead_valid = lead_within[None, :] < usable[:, lead_block]
    lead_local = jax.random.randint(first_key, (PIECES, 4 * HALO), 0, M_DEV)
    leading = jnp.where(lead_valid, M_DEV + lead_block[None, :] * HALO + lead_within[None, :], lead_local)
    remaining = EDGES_DEV - 4 * HALO
    halo_flag = jax.random.randint(flag_key, (PIECES, remaining), 0, 4) == 0
    pick_block = jax.random.randint(block_key, (PIECES, remaining), 0, 4)
    limit = jnp.take_along_axis(usable, pick_block, axis=1)
    pick_within = jax.random.randint(index_key, (PIECES, remaining), 0, 1 << 20) % limit
    rest_local = jax.random.randint(local_key, (PIECES, remaining), 0, M_DEV)
    trailing = jnp.where(halo_flag, M_DEV + pick_block * HALO + pick_within, rest_local)
    slots = jnp.concatenate([leading, trailing], axis=1).astype(jnp.int32)
    shuffle_keys = jax.random.split(order_key, PIECES)
    shuffled = jax.vmap(lambda single, values: jax.random.permutation(single, values))(shuffle_keys, slots)
    return shuffled.reshape(-1).astype(jnp.int32)


def block_levels(key, extent, cuts, smallest, top_value):
    level = 1.0
    for axis_at, parts in cuts:
        heights = jax.random.uniform(jax.random.fold_in(jax.random.fold_in(key, 6), axis_at), (parts,), jnp.float32, smallest / len(cuts), top_value / len(cuts))
        level = level * jnp.repeat(jnp.exp(heights), extent[axis_at] // parts).reshape((-1,) + (1,) * (len(extent) - 1 - axis_at))
    return level


def noise(own_key, extent, width, most, pieces=(), kind=jnp.bfloat16):
    entries = jax.random.normal(own_key, extent, jnp.float32) * width
    if len(pieces) > 0:
        entries = block_levels(own_key, extent, pieces, -0.22, 0.18) * entries
    return jnp.clip(entries, min=-most, max=most).astype(kind)


def setup_inputs(seed: int = 0) -> dict:
    arg_keys = jax.random.split(jax.random.key(seed), 10)
    mesh_latent = noise(arg_keys[0], (DATES, M_ROWS, D), 1.0, 6.0, ((0, 8), (1, 64)))
    grid_latent = noise(arg_keys[1], (DATES, G_ROWS, D), 1.0, 6.0, ((0, 8), (1, 64)))
    cotangent = noise(arg_keys[2], (DATES, G_ROWS, D), 1.0, 6.0, ((0, 8), (1, 64)))
    sender_slot = draw_sender_slot(jax.random.fold_in(arg_keys[9], 71), 0)
    send_rows = draw_send_rows(jax.random.fold_in(arg_keys[9], 71), 0)
    w_send = noise(arg_keys[5], (D, D), D ** -0.5, 0.25)
    w_recv = noise(arg_keys[6], (D, D), D ** -0.5, 0.25)
    w_node = noise(arg_keys[7], (D, D), D ** -0.5, 0.25)
    edge_bias = noise(arg_keys[8], (D,), 0.5, 3.0, (), jnp.float32)
    return dict(mesh_latent=mesh_latent, grid_latent=grid_latent, cotangent=cotangent, sender_slot=sender_slot, send_rows=send_rows, w_send=w_send, w_recv=w_recv, w_node=w_node, edge_bias=edge_bias)


def silu_slope(preact):
    sigmoid_value = jax.nn.sigmoid(preact)
    return sigmoid_value * (1.0 + preact * (1.0 - sigmoid_value))


def reference(mesh_latent, grid_latent, cotangent, sender_slot, send_rows, w_send, w_recv, w_node, edge_bias):
    offset_table = jnp.array([1, -1, STRIDE, PIECES // 2], jnp.int32)
    slots = sender_slot.reshape(PIECES, EDGES_DEV).astype(jnp.int32)
    devices = jnp.arange(PIECES, dtype=jnp.int32)[:, None]
    halo_pos = jnp.clip(slots - M_DEV, 0, 4 * HALO - 1)
    block_index = halo_pos // HALO
    within = halo_pos % HALO
    sources = (devices - offset_table[block_index]) % PIECES
    remote = sources * M_DEV + send_rows[sources, block_index, within]
    senders = jnp.where(slots < M_DEV, devices * M_DEV + slots, remote).reshape(-1).astype(jnp.int32)
    w_send32 = w_send.astype(jnp.float32)

    def one_date(inputs):
        mesh_rows, grid_rows, upstream = inputs
        sent_proj = jnp.dot(mesh_rows, w_send, preferred_element_type=jnp.float32)
        recv_proj = jnp.dot(grid_rows, w_recv, preferred_element_type=jnp.float32)
        preact = sent_proj[senders].reshape(G_ROWS, 3, D) + recv_proj[:, None, :] + edge_bias
        aggregate = jnp.sum(jax.nn.silu(preact), axis=1).astype(jnp.bfloat16)
        agg_grad = jnp.dot(upstream, w_node.T, preferred_element_type=jnp.float32)
        edge_grad = (agg_grad[:, None, :] * silu_slope(preact)).astype(jnp.bfloat16)
        edge_wide = edge_grad.astype(jnp.float32)
        recv_grad = jnp.sum(edge_wide, axis=1).astype(jnp.bfloat16)
        grad_grid = (upstream.astype(jnp.float32) + jnp.dot(recv_grad, w_recv.T, preferred_element_type=jnp.float32)).astype(jnp.bfloat16)
        sender_grad = jax.ops.segment_sum(edge_wide.reshape(EDGES, D), senders, num_segments=M_ROWS)
        grad_mesh = jnp.dot(sender_grad, w_send32.T, precision=lax.Precision.HIGHEST)
        send_term = jnp.dot(mesh_rows.astype(jnp.float32).T, sender_grad, precision=lax.Precision.HIGHEST)
        recv_term = jnp.dot(grid_rows.T, recv_grad, preferred_element_type=jnp.float32)
        node_term = jnp.dot(aggregate.T, upstream, preferred_element_type=jnp.float32)
        bias_term = jnp.sum(edge_wide, axis=(0, 1))
        return grad_mesh, grad_grid, send_term, recv_term, node_term, bias_term

    results = lax.map(one_date, (mesh_latent, grid_latent, cotangent))
    factor = (DATES * G_ROWS) ** -0.5
    grad_w_send = (jnp.sum(results[2], axis=0) * factor).astype(jnp.bfloat16)
    grad_w_recv = (jnp.sum(results[3], axis=0) * factor).astype(jnp.bfloat16)
    grad_w_node = (jnp.sum(results[4], axis=0) * factor).astype(jnp.bfloat16)
    grad_bias = jnp.sum(results[5], axis=0) * factor
    return results[0], results[1], grad_w_send, grad_w_recv, grad_w_node, grad_bias
```

```python
import jax
import jax.numpy as jnp
from jax import lax
from jax.sharding import Mesh, PartitionSpec as P

SPACE = ("y", "x", "core")
BF = jnp.bfloat16
F32 = jnp.float32


def dot_bf16(left, right, left_dim, right_dim):
    return lax.dot_general(
        left.astype(BF),
        right.astype(BF),
        (((left_dim,), (right_dim,)), ((), ())),
        preferred_element_type=F32,
    )


def shift_space(value, offset):
    pieces = lax.axis_size(SPACE)
    return lax.ppermute(value, SPACE, [(i, (i + offset) % pieces) for i in range(pieces)])


def swap_cores(value):
    return lax.ppermute(value, "core", [(0, 1), (1, 0)])


def exchange(value, axes):
    return lax.all_to_all(value, axes, split_axis=0, concat_axis=0, tiled=True)


def gather_pieces(value, axes):
    spread = jnp.broadcast_to(value[None], (lax.axis_size(axes),) + value.shape)
    return exchange(spread, axes)


def reduce_weights(terms, bias, factor):
    core = lax.axis_index("core")
    halves = terms.reshape(2, 768, 512)
    mine = lax.dynamic_index_in_dim(halves, core, 0, keepdims=False)
    other = lax.dynamic_index_in_dim(halves, 1 - core, 0, keepdims=False)
    bias_low = jnp.broadcast_to(bias.astype(BF)[None], (8, 512))
    came = swap_cores(jnp.concatenate([other.astype(BF), bias_low], axis=0)).astype(F32)
    pair = (mine + came[:768]).astype(BF)
    pair_bias = (bias_low.astype(F32) + came[768:]).astype(BF)
    packed = jnp.concatenate(
        [pair.reshape(4, 192, 512), jnp.broadcast_to(pair_bias[None], (4, 8, 512))], axis=1
    )
    line = jnp.sum(exchange(packed, "x").astype(F32), axis=0)
    line_terms = line[:192].astype(BF).reshape(64, 12, 128)
    line_bias = line[192].astype(BF).reshape(1, 4, 128)
    packed = jnp.concatenate(
        [line_terms, jnp.broadcast_to(line_bias, (64, 4, 128))], axis=1
    )
    total = jnp.sum(exchange(packed, ("dp", "y")).astype(F32), axis=0) * factor
    grad_bias = total[12:].reshape(512)
    plane = gather_pieces(total[:12].astype(BF), ("dp", "y")).reshape(192, 512)
    half = gather_pieces(plane, "x").reshape(768, 512)
    partner = swap_cores(half)
    first = jnp.where(core == 0, half, partner)
    second = jnp.where(core == 0, partner, half)
    whole = jnp.concatenate([first, second], axis=0)
    return whole[:512], whole[512:1024], whole[1024:], grad_bias


def per_device(
    mesh_latent, grid_latent, cotangent, sender_slot, send_rows, w_send, w_recv, w_node, edge_bias
):
    mesh_rows = mesh_latent[0]
    grid_rows = grid_latent[0]
    upstream = cotangent[0]
    send_list = send_rows[0]
    count_mesh, width = mesh_rows.shape
    count_grid = grid_rows.shape[0]
    pieces = lax.axis_size(SPACE)
    offsets = (1, -1, max(2, pieces // 8), pieces // 2)
    pick = (
        send_list.reshape(-1)[:, None] == jnp.arange(count_mesh, dtype=jnp.int32)[None, :]
    ).astype(BF)
    outgoing = dot_bf16(pick, mesh_rows, 1, 0).astype(BF).reshape(4, -1, width)
    arrived = [shift_space(outgoing[j], offsets[j]) for j in range(4)]
    recv_proj = dot_bf16(grid_rows, w_recv, 1, 0)
    agg_grad = dot_bf16(upstream, w_node, 1, 1)
    known = jnp.concatenate([mesh_rows] + arrived, axis=0)
    sent_proj = dot_bf16(known, w_send, 1, 0)
    preact = (
        sent_proj[sender_slot].reshape(count_grid, 3, width) + recv_proj[:, None, :] + edge_bias
    )
    sigmoid = jax.nn.sigmoid(preact)
    aggregate = jnp.sum(preact * sigmoid, axis=1).astype(BF)
    slope = sigmoid * (1.0 + preact * (1.0 - sigmoid))
    edge_grad = (agg_grad[:, None, :] * slope).astype(BF)
    edge_flat = edge_grad.reshape(-1, width)
    recv_grad = jnp.sum(edge_grad, axis=1, dtype=F32).astype(BF)
    slot_table = (
        sender_slot[:, None] == jnp.arange(known.shape[0], dtype=jnp.int32)[None, :]
    ).astype(BF)
    slot_grad = dot_bf16(slot_table, edge_flat, 0, 0)
    send_term = dot_bf16(known, slot_grad, 0, 0)
    recv_term = dot_bf16(grid_rows, recv_grad, 0, 0)
    node_term = dot_bf16(aggregate, upstream, 0, 0)
    bias_term = jnp.sum(edge_flat, axis=0, dtype=F32)
    factor = float(lax.axis_size("dp") * pieces * count_grid) ** (-0.5)
    grad_w_send, grad_w_recv, grad_w_node, grad_bias = reduce_weights(
        jnp.concatenate([send_term, recv_term, node_term], axis=0), bias_term, factor
    )
    leaving = slot_grad[count_mesh:].astype(BF).reshape(4, -1, width)
    returned = jnp.concatenate(
        [shift_space(leaving[j], -offsets[j]) for j in range(4)], axis=0
    )
    sender_grad = slot_grad[:count_mesh] + dot_bf16(pick, returned, 0, 0)
    grad_mesh = dot_bf16(sender_grad, w_send, 1, 1)
    grad_grid = (upstream.astype(F32) + dot_bf16(recv_grad, w_recv, 1, 1)).astype(BF)
    return (grad_mesh[None], grad_grid[None], grad_w_send, grad_w_recv, grad_w_node, grad_bias)


def solution(mesh):
    fine = Mesh(mesh.devices.reshape(8, 8, 4, 2), ("dp",) + SPACE)
    placed = (
        P("dp", SPACE, None),
        P("dp", SPACE, None),
        P("dp", SPACE, None),
        P(SPACE),
        P(SPACE, None, None),
        P(),
        P(),
        P(),
        P(),
    )
    return jax.shard_map(
        per_device,
        mesh=fine,
        in_specs=placed,
        out_specs=(P("dp", SPACE, None), P("dp", SPACE, None), P(), P(), P(), P()),
        check_vma=False,
    )
```

```python
import jax
import jax.numpy as jnp
from jax import lax
from jax.experimental import pallas as pl
from jax.experimental.pallas import tpu as pltpu
from jax.sharding import Mesh, PartitionSpec as P

BF = jnp.bfloat16
F32 = jnp.float32


def rows_dot(left, right):
    return lax.dot_general(left, right, (((0,), (0,)), ((), ())), preferred_element_type=F32)


def half_terms(start, known_ref, slot_ref, grid_ref, recv_ref, node_ref, upstream_ref, out_ref):
    span = pl.ds(pl.multiple_of(start, 256), 256)
    pairs = ((known_ref, slot_ref), (grid_ref, recv_ref), (node_ref, upstream_ref))
    for index, (left_ref, right_ref) in enumerate(pairs):
        product = rows_dot(left_ref[:, span], right_ref[...])
        out_ref[index * 256 : (index + 1) * 256, :] = product.astype(out_ref.dtype)


def edge_kernel(
    core_ref, column_ref, row_ref, mesh_ref, h0_ref, h1_ref, h2_ref, h3_ref, recv_proj_ref, agg_grad_ref,
    w_send_ref, grid_ref, upstream_ref,
    send_ref, known_ref, slot_ref, recv_ref, node_ref, local_ref,
    table_ref, preact_ref, edge_ref, bias_ref,
):
    known_ref[0:128, :] = mesh_ref[...]
    for j, halo_ref in enumerate((h0_ref, h1_ref, h2_ref, h3_ref)):
        known_ref[128 + 16 * j : 144 + 16 * j, :] = halo_ref[...]
    sent = jnp.dot(known_ref[...], w_send_ref[...], preferred_element_type=F32)
    high = sent.astype(BF)
    table_ref[0:192, :] = high
    table_ref[192:384, :] = (sent - high.astype(F32)).astype(BF)
    lane = lax.broadcasted_iota(jnp.int32, (512, 384), 1)
    lane = jnp.where(lane >= 192, lane - 192, lane)
    for k in range(3):
        pick = (lane == column_ref[:, k : k + 1]).astype(F32).astype(BF)
        preact_ref[k * 512 : (k + 1) * 512, :] = jnp.dot(
            pick, table_ref[...], preferred_element_type=F32
        )
    bias_ref[...] = jnp.zeros_like(bias_ref)

    def chunk(step, carry):
        rows = pl.ds(pl.multiple_of(step * 16, 16), 16)
        recv_proj = recv_proj_ref[rows, :]
        agg_grad = agg_grad_ref[rows, :]
        node = jnp.zeros((16, 512), F32)
        recv = jnp.zeros((16, 512), F32)
        for k in range(3):
            edge_rows = pl.ds(pl.multiple_of(step * 16 + k * 512, 16), 16)
            preact = preact_ref[edge_rows, :] + recv_proj
            sigmoid = 0.5 * jnp.tanh(0.5 * preact) + 0.5
            silu = preact * sigmoid
            node += silu
            edge = (agg_grad * (sigmoid + silu * (1.0 - sigmoid))).astype(BF)
            edge_ref[edge_rows, :] = edge
            recv += edge.astype(F32)
        node_ref[rows, :] = node.astype(BF)
        recv_ref[rows, :] = recv.astype(BF)
        bias_ref[...] += recv[0:8] + recv[8:16]
        return carry

    lax.fori_loop(0, 32, chunk, 0)
    sublane = lax.broadcasted_iota(jnp.int32, (192, 1536), 0)
    spread = (sublane == row_ref[...]).astype(F32).astype(BF)
    slots = jnp.dot(spread, edge_ref[...], preferred_element_type=F32)
    local_ref[...] = slots[0:128]
    slot_ref[...] = slots.astype(BF)
    half_terms((1 - core_ref[0]) * 256, known_ref, slot_ref, grid_ref, recv_ref, node_ref, upstream_ref, send_ref)
    total = jnp.sum(bias_ref[...], axis=0, keepdims=True)
    send_ref[768:784, :] = jnp.broadcast_to(total, (16, 512)).astype(BF)
    leaving = pl.ds(pl.multiple_of(144 - 16 * core_ref[0], 16), 16)
    send_ref[784:800, :] = slot_ref[leaving, :]


def keep_kernel(core_ref, known_ref, slot_ref, grid_ref, recv_ref, node_ref, upstream_ref, keep_ref):
    half_terms(core_ref[0] * 256, known_ref, slot_ref, grid_ref, recv_ref, node_ref, upstream_ref, keep_ref)


VM = pl.BlockSpec(memory_space=pltpu.VMEM)
SM = pl.BlockSpec(memory_space=pltpu.SMEM)
LIMIT = pltpu.CompilerParams(vmem_limit_bytes=40 * 1024 * 1024)


def pack_kernel(keep_ref, came_ref, sent_ref, out_ref):
    bias = (sent_ref[...].astype(F32) + came_ref[768:784, :].astype(F32)).astype(BF)
    for piece in range(4):
        rows = slice(piece * 192, piece * 192 + 192)
        out_ref[piece, 0:192, :] = (keep_ref[rows, :] + came_ref[rows, :].astype(F32)).astype(BF)
        out_ref[piece, 192:208, :] = bias


def shape(rows, dtype):
    return jax.ShapeDtypeStruct((rows, 512), dtype)


def edge_step(*args):
    return pl.pallas_call(
        edge_kernel,
        out_shape=(shape(800, BF), shape(192, BF), shape(192, BF), shape(512, BF), shape(512, BF), shape(128, F32)),
        in_specs=[SM] + [VM] * 12,
        out_specs=(VM,) * 6,
        scratch_shapes=[
            pltpu.VMEM((384, 512), BF),
            pltpu.VMEM((1536, 512), F32),
            pltpu.VMEM((1536, 512), BF),
            pltpu.VMEM((8, 512), F32),
        ],
        compiler_params=LIMIT,
        name="edge_step",
        cost_estimate=pl.CostEstimate(flops=3_000_000_000, bytes_accessed=6_000_000, transcendentals=800_000),
    )(*args)


def keep_step(*args):
    return pl.pallas_call(
        keep_kernel,
        out_shape=shape(768, F32),
        in_specs=[SM] + [VM] * 6,
        out_specs=VM,
        compiler_params=LIMIT,
        name="keep_step",
        cost_estimate=pl.CostEstimate(flops=600_000_000, bytes_accessed=4_000_000, transcendentals=0),
    )(*args)


def pack_step(*args):
    return pl.pallas_call(
        pack_kernel,
        out_shape=jax.ShapeDtypeStruct((4, 208, 512), BF),
        in_specs=[VM] * 3,
        out_specs=VM,
        compiler_params=LIMIT,
        name="pack_step",
        cost_estimate=pl.CostEstimate(flops=500_000, bytes_accessed=3_000_000, transcendentals=0),
    )(*args)


SPACE = ("y", "x", "core")
PLANE = ("dp", "y")


def dot_bf16(left, right, left_dim, right_dim):
    return lax.dot_general(
        left.astype(BF),
        right.astype(BF),
        (((left_dim,), (right_dim,)), ((), ())),
        preferred_element_type=F32,
    )


def shift_space(value, offset):
    pieces = lax.axis_size(SPACE)
    return lax.ppermute(value, SPACE, [(i, (i + offset) % pieces) for i in range(pieces)])


def swap_chips(value):
    pieces = lax.axis_size(SPACE)
    return lax.ppermute(
        value, SPACE, [(i, (i - 1 + 2 * (i % 2)) % pieces) for i in range(pieces)]
    )


def swap_cores(value):
    return lax.ppermute(value, "core", [(0, 1), (1, 0)])


def exchange(value, axes):
    return lax.all_to_all(value, axes, split_axis=0, concat_axis=0, tiled=True)


def gather_pieces(value, axes):
    spread = jnp.broadcast_to(value[None], (lax.axis_size(axes),) + value.shape)
    return exchange(spread, axes)


def per_device(
    mesh_latent, grid_latent, cotangent, sender_slot, send_rows, w_send, w_recv, w_node, edge_bias
):
    mesh_rows = mesh_latent[0]
    grid_rows = grid_latent[0]
    upstream = cotangent[0]
    core = lax.axis_index("core")
    core_ref = core.astype(jnp.int32).reshape(1)
    pieces = lax.axis_size(SPACE)
    offsets = (1, -1, max(2, pieces // 8), pieces // 2)
    pick = (
        send_rows[0].reshape(-1)[:, None] == jnp.arange(128, dtype=jnp.int32)[None, :]
    ).astype(BF)
    outgoing = dot_bf16(pick, mesh_rows, 1, 0).astype(BF).reshape(4, 16, 512)
    halo = [shift_space(outgoing[j], offsets[j]) for j in range(4)]
    recv_proj = dot_bf16(grid_rows, w_recv, 1, 0) + edge_bias
    agg_grad = dot_bf16(upstream, w_node, 1, 1)
    column = sender_slot.reshape(512, 3)
    row = column.T.reshape(1, 1536)
    send, known, slot, recv_grad, node, local = edge_step(
        core_ref, column, row, mesh_rows, *halo, recv_proj, agg_grad, w_send, grid_rows, upstream
    )
    came = swap_cores(send)
    keep = keep_step(core_ref, known, slot, grid_rows, recv_grad, node, upstream)
    packed = pack_step(keep, came, send[768:784])

    line = jnp.sum(exchange(packed, "x").astype(F32), axis=0)
    line_terms = line[:192].astype(BF).reshape(64, 12, 128)
    line_bias = line[192].astype(BF).reshape(1, 4, 128)
    packed = jnp.concatenate([line_terms, jnp.broadcast_to(line_bias, (64, 4, 128))], axis=1)
    factor = float(lax.axis_size("dp") * pieces * 512) ** (-0.5)
    total = jnp.sum(exchange(packed, PLANE).astype(F32), axis=0) * factor
    grad_bias = total[12:].reshape(512)
    plane = gather_pieces(total[:12].astype(BF), PLANE).reshape(192, 512)

    near = came[784:800]
    next_chip = swap_chips(jnp.where(core == 0, slot[128:144], slot[144:160]))
    far = [shift_space(slot[128 + 16 * j : 144 + 16 * j], -offsets[j]) for j in (2, 3)]
    first = jnp.where(core == 0, near, next_chip)
    second = jnp.where(core == 0, next_chip, near)
    returned = jnp.concatenate([first, second] + far, axis=0)
    grad_mesh = dot_bf16(local + dot_bf16(pick, returned, 0, 0), w_send, 1, 1)
    grad_grid = (upstream.astype(F32) + dot_bf16(recv_grad, w_recv, 1, 1)).astype(BF)
    plane, grad_mesh, grad_grid = lax.optimization_barrier((plane, grad_mesh, grad_grid))

    half = gather_pieces(plane, "x").reshape(3, 1, 256, 512)
    partner = swap_cores(half)
    low = jnp.where(core == 0, half, partner)
    high = jnp.where(core == 0, partner, half)
    whole = jnp.concatenate([low, high], axis=1).reshape(3, 512, 512)
    return (grad_mesh[None], grad_grid[None], whole[0], whole[1], whole[2], grad_bias)


def solution(mesh):
    fine = Mesh(mesh.devices.reshape(8, 8, 4, 2), ("dp",) + SPACE)
    placed = (
        P("dp", SPACE, None),
        P("dp", SPACE, None),
        P("dp", SPACE, None),
        P(SPACE),
        P(SPACE, None, None),
        P(),
        P(),
        P(),
        P(),
    )
    return jax.shard_map(
        per_device,
        mesh=fine,
        in_specs=placed,
        out_specs=(P("dp", SPACE, None), P("dp", SPACE, None), P(), P(), P(), P()),
        check_vma=False,
    )
```

```python
import jax
import jax.numpy as jnp
from jax import lax
from jax.experimental import pallas as pl
from jax.experimental.pallas import tpu as pltpu
from jax.sharding import Mesh, PartitionSpec as P

BF = jnp.bfloat16
F32 = jnp.float32


def rows_dot(left, right):
    return lax.dot_general(left, right, (((0,), (0,)), ((), ())), preferred_element_type=F32)


def half_terms(start, known_ref, slot_ref, grid_ref, recv_ref, node_ref, upstream_ref, out_ref):
    span = pl.ds(pl.multiple_of(start, 256), 256)
    pairs = ((known_ref, slot_ref), (grid_ref, recv_ref), (node_ref, upstream_ref))
    for index, (left_ref, right_ref) in enumerate(pairs):
        product = rows_dot(left_ref[:, span], right_ref[...])
        out_ref[index * 256 : (index + 1) * 256, :] = product.astype(out_ref.dtype)


def pick_kernel(rows_hbm, mesh_hbm, o0_ref, o1_ref, o2_ref, o3_ref, rows_ref, mesh_ref, arrived):
    mesh_copy = pltpu.make_async_copy(mesh_hbm, mesh_ref, arrived.at[0])
    rows_copy = pltpu.make_async_copy(rows_hbm, rows_ref, arrived.at[1])
    mesh_copy.start()
    rows_copy.start()
    rows_copy.wait()
    mesh_copy.wait()
    sublane = lax.broadcasted_iota(jnp.int32, (128, 16), 0)
    for j, out_ref in enumerate((o0_ref, o1_ref, o2_ref, o3_ref)):
        pick = (sublane == rows_ref[j : j + 1, :]).astype(F32).astype(BF)
        out_ref[...] = rows_dot(pick, mesh_ref[...]).astype(BF)


def edge_kernel(
    core_ref, column_ref, row_ref, mesh_ref, grid_ref, upstream_ref,
    h0_ref, h1_ref, h2_ref, h3_ref, w_hbm, recv_proj_hbm, agg_grad_hbm,
    send_ref, known_ref, slot_ref, recv_ref, node_ref, local_ref, next_ref, far_ref, last_ref,
    table_ref, preact_ref, edge_ref, bias_ref, w_send_ref, recv_proj_ref, agg_grad_ref, arrived,
):
    copies = [
        pltpu.make_async_copy(halo_ref, known_ref.at[pl.ds(128 + 16 * j, 16)], arrived.at[j])
        for j, halo_ref in enumerate((h0_ref, h1_ref, h2_ref, h3_ref))
    ]
    copies.append(pltpu.make_async_copy(w_hbm, w_send_ref, arrived.at[4]))
    copies.append(pltpu.make_async_copy(recv_proj_hbm, recv_proj_ref, arrived.at[5]))
    copies.append(pltpu.make_async_copy(agg_grad_hbm, agg_grad_ref, arrived.at[6]))
    for copy in copies:
        copy.start()
    known_ref[0:128, :] = mesh_ref[...]
    for copy in copies[:5]:
        copy.wait()
    sent = jnp.dot(known_ref[...], w_send_ref[...], preferred_element_type=F32)
    high = sent.astype(BF)
    table_ref[0:192, :] = high
    table_ref[192:384, :] = (sent - high.astype(F32)).astype(BF)
    lane = lax.broadcasted_iota(jnp.int32, (512, 384), 1)
    lane = jnp.where(lane >= 192, lane - 192, lane)
    for k in range(3):
        pick = (lane == column_ref[:, k : k + 1]).astype(F32).astype(BF)
        preact_ref[k * 512 : (k + 1) * 512, :] = jnp.dot(
            pick, table_ref[...], preferred_element_type=F32
        )
    copies[5].wait()
    copies[6].wait()
    bias_ref[...] = jnp.zeros_like(bias_ref)

    def chunk(step, carry):
        rows = pl.ds(pl.multiple_of(step * 16, 16), 16)
        recv_proj = recv_proj_ref[rows, :]
        agg_grad = agg_grad_ref[rows, :]
        node = jnp.zeros((16, 512), F32)
        recv = jnp.zeros((16, 512), F32)
        for k in range(3):
            edge_rows = pl.ds(pl.multiple_of(step * 16 + k * 512, 16), 16)
            preact = preact_ref[edge_rows, :] + recv_proj
            sigmoid = 0.5 * jnp.tanh(0.5 * preact) + 0.5
            silu = preact * sigmoid
            node += silu
            edge = (agg_grad * (sigmoid + silu * (1.0 - sigmoid))).astype(BF)
            edge_ref[edge_rows, :] = edge
            recv += edge.astype(F32)
        node_ref[rows, :] = node.astype(BF)
        recv_ref[rows, :] = recv.astype(BF)
        bias_ref[...] += recv[0:8] + recv[8:16]
        return carry

    lax.fori_loop(0, 32, chunk, 0)
    sublane = lax.broadcasted_iota(jnp.int32, (192, 1536), 0)
    spread = (sublane == row_ref[...]).astype(F32).astype(BF)
    slots = jnp.dot(spread, edge_ref[...], preferred_element_type=F32)
    local_ref[...] = slots[0:128]
    slot_ref[...] = slots.astype(BF)
    half_terms((1 - core_ref[0]) * 256, known_ref, slot_ref, grid_ref, recv_ref, node_ref, upstream_ref, send_ref)
    total = jnp.sum(bias_ref[...], axis=0, keepdims=True)
    send_ref[768:784, :] = jnp.broadcast_to(total, (16, 512)).astype(BF)
    leaving = pl.ds(pl.multiple_of(144 - 16 * core_ref[0], 16), 16)
    send_ref[784:800, :] = slot_ref[leaving, :]
    staying = pl.ds(pl.multiple_of(128 + 16 * core_ref[0], 16), 16)
    next_ref[...] = slot_ref[staying, :]
    far_ref[...] = slot_ref[160:176, :]
    last_ref[...] = slot_ref[176:192, :]


def keep_kernel(core_ref, known_ref, slot_ref, grid_ref, recv_ref, node_ref, upstream_ref, keep_ref):
    half_terms(core_ref[0] * 256, known_ref, slot_ref, grid_ref, recv_ref, node_ref, upstream_ref, keep_ref)


VM = pl.BlockSpec(memory_space=pltpu.VMEM)
HBM = pl.BlockSpec(memory_space=pltpu.HBM)
SM = pl.BlockSpec(memory_space=pltpu.SMEM)


def limit(mebibytes):
    return pltpu.CompilerParams(vmem_limit_bytes=mebibytes * 1024 * 1024)


def pack_kernel(keep_ref, came_ref, sent_ref, out_ref, near_ref):
    near_ref[...] = came_ref[784:800, :]
    bias = (sent_ref[...].astype(F32) + came_ref[768:784, :].astype(F32)).astype(BF)
    for piece in range(4):
        rows = slice(piece * 192, piece * 192 + 192)
        out_ref[piece, 0:192, :] = (keep_ref[rows, :] + came_ref[rows, :].astype(F32)).astype(BF)
        out_ref[piece, 192:208, :] = bias


def line_kernel(packed_hbm, out_ref, packed_ref, line_ref, bias_ref, arrived):
    copies = [
        pltpu.make_async_copy(packed_hbm.at[piece], packed_ref.at[piece], arrived.at[piece])
        for piece in range(4)
    ]
    for copy in copies:
        copy.start()
    for copy in copies:
        copy.wait()
    line_ref[...] = sum(packed_ref[piece].astype(F32) for piece in range(4))
    bias = line_ref[192:193, :]
    for j in range(4):
        bias_ref[12 + j : 13 + j, :] = bias[:, 128 * j : 128 * j + 128]
    sublane = lax.broadcasted_iota(jnp.int32, (16, 128), 0)
    for piece in range(64):
        top, left = 12 * (piece // 4), 128 * (piece % 4)
        tile = jnp.where(sublane < 12, line_ref[top : top + 16, left : left + 128], bias_ref[...])
        out_ref[piece] = tile.astype(BF)


def tail_kernel(
    core_ref, rows_ref, local_ref, near_ref, next_ref, far_ref, last_ref, w_send_ref,
    upstream_ref, recv_ref, w_recv_ref, mesh_ref, grid_ref,
):
    product = lax.dot_general(
        recv_ref[...], w_recv_ref[...], (((1,), (1,)), ((), ())), preferred_element_type=F32
    )
    grid_ref[...] = (upstream_ref[...].astype(F32) + product).astype(BF)
    first_core = core_ref[0] == 0
    near, other = near_ref[...], next_ref[...]
    blocks = (
        jnp.where(first_core, near, other),
        jnp.where(first_core, other, near),
        far_ref[...],
        last_ref[...],
    )
    sublane = lax.broadcasted_iota(jnp.int32, (128, 16), 0)
    grad = local_ref[...]
    for j, block in enumerate(blocks):
        pick = (sublane == rows_ref[j : j + 1, :]).astype(F32).astype(BF)
        grad += jnp.dot(pick, block, preferred_element_type=F32)
    mesh_ref[...] = lax.dot_general(
        grad.astype(BF), w_send_ref[...], (((1,), (1,)), ((), ())), preferred_element_type=F32
    )


def shape(rows, dtype):
    return jax.ShapeDtypeStruct((rows, 512), dtype)


def edge_step(*args):
    return pl.pallas_call(
        edge_kernel,
        out_shape=(shape(800, BF), shape(192, BF), shape(192, BF), shape(512, BF), shape(512, BF), shape(128, F32))
        + (shape(16, BF),) * 3,
        in_specs=[SM] + [VM] * 5 + [HBM] * 7,
        out_specs=(VM,) * 9,
        scratch_shapes=[
            pltpu.VMEM((384, 512), BF),
            pltpu.VMEM((1536, 512), F32),
            pltpu.VMEM((1536, 512), BF),
            pltpu.VMEM((8, 512), F32),
            pltpu.VMEM((512, 512), BF),
            pltpu.VMEM((512, 512), F32),
            pltpu.VMEM((512, 512), F32),
            pltpu.SemaphoreType.DMA((7,)),
        ],
        compiler_params=limit(24),
        name="edge_step",
        cost_estimate=pl.CostEstimate(flops=3_000_000_000, bytes_accessed=6_000_000, transcendentals=800_000),
    )(*args)


def keep_step(*args):
    return pl.pallas_call(
        keep_kernel,
        out_shape=shape(768, F32),
        in_specs=[SM] + [VM] * 6,
        out_specs=VM,
        compiler_params=limit(10),
        name="keep_step",
        cost_estimate=pl.CostEstimate(flops=600_000_000, bytes_accessed=4_000_000, transcendentals=0),
    )(*args)


def pack_step(*args):
    return pl.pallas_call(
        pack_kernel,
        out_shape=(jax.ShapeDtypeStruct((4, 208, 512), BF), shape(16, BF)),
        in_specs=[VM] * 3,
        out_specs=(VM,) * 2,
        compiler_params=limit(8),
        name="pack_step",
        cost_estimate=pl.CostEstimate(flops=500_000, bytes_accessed=3_000_000, transcendentals=0),
    )(*args)


def pick_step(*args):
    return pl.pallas_call(
        pick_kernel,
        out_shape=(shape(16, BF),) * 4,
        in_specs=[HBM] * 2,
        out_specs=(VM,) * 4,
        scratch_shapes=[
            pltpu.VMEM((4, 16), jnp.int32),
            pltpu.VMEM((128, 512), BF),
            pltpu.SemaphoreType.DMA((2,)),
        ],
        name="pick_step",
        cost_estimate=pl.CostEstimate(flops=10_000_000, bytes_accessed=200_000, transcendentals=0),
    )(*args)


def line_step(packed):
    return pl.pallas_call(
        line_kernel,
        out_shape=jax.ShapeDtypeStruct((64, 16, 128), BF),
        in_specs=[HBM],
        out_specs=VM,
        scratch_shapes=[
            pltpu.VMEM((4, 208, 512), BF),
            pltpu.VMEM((208, 512), F32),
            pltpu.VMEM((16, 128), F32),
            pltpu.SemaphoreType.DMA((4,)),
        ],
        compiler_params=limit(8),
        name="line_step",
        cost_estimate=pl.CostEstimate(flops=500_000, bytes_accessed=1_000_000, transcendentals=0),
    )(packed)


def tail_step(*args):
    return pl.pallas_call(
        tail_kernel,
        out_shape=(shape(128, F32), shape(512, BF)),
        in_specs=[SM] + [VM] * 10,
        out_specs=(VM,) * 2,
        compiler_params=limit(8),
        name="tail_step",
        cost_estimate=pl.CostEstimate(flops=400_000_000, bytes_accessed=3_000_000, transcendentals=0),
    )(*args)


SPACE = ("y", "x", "core")
PLANE = ("dp", "y")


def shift_space(value, offset):
    pieces = lax.axis_size(SPACE)
    return lax.ppermute(value, SPACE, [(i, (i + offset) % pieces) for i in range(pieces)])


def swap_chips(value):
    pieces = lax.axis_size(SPACE)
    return lax.ppermute(
        value, SPACE, [(i, (i - 1 + 2 * (i % 2)) % pieces) for i in range(pieces)]
    )


def swap_cores(value):
    return lax.ppermute(value, "core", [(0, 1), (1, 0)])


def exchange(value, axes):
    return lax.all_to_all(value, axes, split_axis=0, concat_axis=0, tiled=True)


def gather_pieces(value, axes):
    spread = jnp.broadcast_to(value[None], (lax.axis_size(axes),) + value.shape)
    return exchange(spread, axes)


def per_device(
    mesh_latent, grid_latent, cotangent, sender_slot, send_rows, w_send, w_recv, w_node, edge_bias
):
    mesh_rows = mesh_latent[0]
    grid_rows = grid_latent[0]
    upstream = cotangent[0]
    core = lax.axis_index("core")
    core_ref = core.astype(jnp.int32).reshape(1)
    pieces = lax.axis_size(SPACE)
    offsets = (1, -1, max(2, pieces // 8), pieces // 2)
    outgoing = pick_step(send_rows[0], mesh_rows)
    halo = [shift_space(outgoing[j], offsets[j]) for j in range(4)]
    recv_proj = lax.dot_general(
        grid_rows, w_recv, (((1,), (0,)), ((), ())), preferred_element_type=F32
    ) + edge_bias
    agg_grad = lax.dot_general(
        upstream, w_node, (((1,), (1,)), ((), ())), preferred_element_type=F32
    )
    column = sender_slot.reshape(512, 3)
    row = column.T.reshape(1, 1536)
    send, known, slot, recv_grad, node, local, *leaving = edge_step(
        core_ref, column, row, mesh_rows, grid_rows, upstream, *halo, w_send, recv_proj, agg_grad
    )
    came = swap_cores(send)
    keep = keep_step(core_ref, known, slot, grid_rows, recv_grad, node, upstream)
    packed, near = pack_step(keep, came, send[768:784])
    packed, *leaving = lax.optimization_barrier((packed, *leaving))

    next_chip = swap_chips(leaving[0])
    far = shift_space(leaving[1], -offsets[2])
    last = shift_space(leaving[2], -offsets[3])
    line = line_step(exchange(packed, "x"))
    line, next_chip, far, last = lax.optimization_barrier((line, next_chip, far, last))

    factor = float(lax.axis_size("dp") * pieces * 512) ** (-0.5)
    total = jnp.sum(exchange(line, PLANE).astype(F32), axis=0) * factor
    grad_bias = total[12:].reshape(512)
    plane = gather_pieces(total.astype(BF), PLANE)[:, :12].reshape(16, 4, 12, 128)
    plane = plane.transpose(0, 2, 1, 3).reshape(192, 512)
    grad_mesh, grad_grid = tail_step(
        core_ref, send_rows[0], local, near, next_chip, far, last, w_send, upstream, recv_grad, w_recv
    )
    plane, grad_mesh, grad_grid, grad_bias = lax.optimization_barrier(
        (plane, grad_mesh, grad_grid, grad_bias)
    )

    half = gather_pieces(plane, "x").reshape(3, 1, 256, 512)
    partner = swap_cores(half)
    low = jnp.where(core == 0, half, partner)
    high = jnp.where(core == 0, partner, half)
    whole = jnp.concatenate([low, high], axis=1).reshape(3, 512, 512)
    return (grad_mesh[None], grad_grid[None], whole[0], whole[1], whole[2], grad_bias)


def solution(mesh):
    fine = Mesh(mesh.devices.reshape(8, 8, 4, 2), ("dp",) + SPACE)
    placed = (
        P("dp", SPACE, None),
        P("dp", SPACE, None),
        P("dp", SPACE, None),
        P(SPACE),
        P(SPACE, None, None),
        P(),
        P(),
        P(),
        P(),
    )
    return jax.shard_map(
        per_device,
        mesh=fine,
        in_specs=placed,
        out_specs=(P("dp", SPACE, None), P("dp", SPACE, None), P(), P(), P(), P()),
        check_vma=False,
    )
```

```python
import jax
import jax.numpy as jnp
from jax import lax
from jax.experimental import pallas as pl
from jax.experimental.pallas import tpu as pltpu
from jax.sharding import Mesh, PartitionSpec as P

BF = jnp.bfloat16
F32 = jnp.float32


def rows_dot(left, right):
    return lax.dot_general(left, right, (((0,), (0,)), ((), ())), preferred_element_type=F32)


def half_terms(start, known_ref, slot_ref, grid_ref, recv_ref, node_ref, upstream_ref, out_ref):
    span = pl.ds(pl.multiple_of(start, 256), 256)
    pairs = ((known_ref, slot_ref), (grid_ref, recv_ref), (node_ref, upstream_ref))
    for index, (left_ref, right_ref) in enumerate(pairs):
        product = rows_dot(left_ref[:, span], right_ref[...])
        out_ref[index * 256 : (index + 1) * 256, :] = product.astype(out_ref.dtype)


def pick_kernel(rows_hbm, mesh_hbm, o0_ref, o1_ref, o2_ref, o3_ref, rows_ref, mesh_ref, arrived):
    mesh_copy = pltpu.make_async_copy(mesh_hbm, mesh_ref, arrived.at[0])
    rows_copy = pltpu.make_async_copy(rows_hbm, rows_ref, arrived.at[1])
    mesh_copy.start()
    rows_copy.start()
    rows_copy.wait()
    mesh_copy.wait()
    sublane = lax.broadcasted_iota(jnp.int32, (128, 16), 0)
    for j, out_ref in enumerate((o0_ref, o1_ref, o2_ref, o3_ref)):
        pick = (sublane == rows_ref[j : j + 1, :]).astype(F32).astype(BF)
        out_ref[...] = rows_dot(pick, mesh_ref[...]).astype(BF)


def edge_kernel(
    core_ref, column_ref, row_ref, mesh_ref, grid_ref, upstream_ref,
    h0_ref, h1_ref, h2_ref, h3_ref, w_hbm, recv_proj_hbm, agg_grad_hbm,
    send_ref, known_ref, slot_ref, recv_ref, node_ref, local_ref, next_ref, far_ref, last_ref,
    table_ref, preact_ref, edge_ref, bias_ref, w_send_ref, recv_proj_ref, agg_grad_ref, arrived,
):
    copies = [
        pltpu.make_async_copy(halo_ref, known_ref.at[pl.ds(128 + 16 * j, 16)], arrived.at[j])
        for j, halo_ref in enumerate((h0_ref, h1_ref, h2_ref, h3_ref))
    ]
    copies.append(pltpu.make_async_copy(w_hbm, w_send_ref, arrived.at[4]))
    copies.append(pltpu.make_async_copy(recv_proj_hbm, recv_proj_ref, arrived.at[5]))
    copies.append(pltpu.make_async_copy(agg_grad_hbm, agg_grad_ref, arrived.at[6]))
    for copy in copies:
        copy.start()
    known_ref[0:128, :] = mesh_ref[...]
    for copy in copies[:5]:
        copy.wait()
    sent = jnp.dot(known_ref[...], w_send_ref[...], preferred_element_type=F32)
    high = sent.astype(BF)
    table_ref[0:192, :] = high
    table_ref[192:384, :] = (sent - high.astype(F32)).astype(BF)
    lane = lax.broadcasted_iota(jnp.int32, (512, 384), 1)
    lane = jnp.where(lane >= 192, lane - 192, lane)
    for k in range(3):
        pick = (lane == column_ref[:, k : k + 1]).astype(F32).astype(BF)
        preact_ref[k * 512 : (k + 1) * 512, :] = jnp.dot(
            pick, table_ref[...], preferred_element_type=F32
        )
    copies[5].wait()
    copies[6].wait()
    bias_ref[...] = jnp.zeros_like(bias_ref)

    def chunk(step, carry):
        rows = pl.ds(pl.multiple_of(step * 16, 16), 16)
        recv_proj = recv_proj_ref[rows, :]
        agg_grad = agg_grad_ref[rows, :]
        node = jnp.zeros((16, 512), F32)
        recv = jnp.zeros((16, 512), F32)
        for k in range(3):
            edge_rows = pl.ds(pl.multiple_of(step * 16 + k * 512, 16), 16)
            preact = preact_ref[edge_rows, :] + recv_proj
            sigmoid = 0.5 * jnp.tanh(0.5 * preact) + 0.5
            silu = preact * sigmoid
            node += silu
            edge = (agg_grad * (sigmoid + silu * (1.0 - sigmoid))).astype(BF)
            edge_ref[edge_rows, :] = edge
            recv += edge.astype(F32)
        node_ref[rows, :] = node.astype(BF)
        recv_ref[rows, :] = recv.astype(BF)
        bias_ref[...] += recv[0:8] + recv[8:16]
        return carry

    lax.fori_loop(0, 32, chunk, 0)
    sublane = lax.broadcasted_iota(jnp.int32, (192, 1536), 0)
    spread = (sublane == row_ref[...]).astype(F32).astype(BF)
    slots = jnp.dot(spread, edge_ref[...], preferred_element_type=F32)
    local_ref[...] = slots[0:128]
    slot_ref[...] = slots.astype(BF)
    half_terms((1 - core_ref[0]) * 256, known_ref, slot_ref, grid_ref, recv_ref, node_ref, upstream_ref, send_ref)
    total = jnp.sum(bias_ref[...], axis=0, keepdims=True)
    send_ref[768:784, :] = jnp.broadcast_to(total, (16, 512)).astype(BF)
    leaving = pl.ds(pl.multiple_of(144 - 16 * core_ref[0], 16), 16)
    send_ref[784:800, :] = slot_ref[leaving, :]
    staying = pl.ds(pl.multiple_of(128 + 16 * core_ref[0], 16), 16)
    next_ref[...] = slot_ref[staying, :]
    far_ref[...] = slot_ref[160:176, :]
    last_ref[...] = slot_ref[176:192, :]


def keep_kernel(core_ref, known_ref, slot_ref, grid_ref, recv_ref, node_ref, upstream_ref, keep_ref):
    half_terms(core_ref[0] * 256, known_ref, slot_ref, grid_ref, recv_ref, node_ref, upstream_ref, keep_ref)


VM = pl.BlockSpec(memory_space=pltpu.VMEM)
HBM = pl.BlockSpec(memory_space=pltpu.HBM)
SM = pl.BlockSpec(memory_space=pltpu.SMEM)


def limit(mebibytes):
    return pltpu.CompilerParams(vmem_limit_bytes=mebibytes * 1024 * 1024)


def pack_kernel(keep_ref, came_ref, sent_ref, out_ref, near_ref):
    near_ref[...] = came_ref[784:800, :]
    bias = (sent_ref[...].astype(F32) + came_ref[768:784, :].astype(F32)).astype(BF)
    for piece in range(4):
        rows = slice(piece * 192, piece * 192 + 192)
        out_ref[piece, 0:192, :] = (keep_ref[rows, :] + came_ref[rows, :].astype(F32)).astype(BF)
        out_ref[piece, 192:208, :] = bias


def line_kernel(packed_hbm, out_ref, packed_ref, line_ref, bias_ref, arrived):
    copies = [
        pltpu.make_async_copy(packed_hbm.at[piece], packed_ref.at[piece], arrived.at[piece])
        for piece in range(4)
    ]
    for copy in copies:
        copy.start()
    for copy in copies:
        copy.wait()
    line_ref[...] = sum(packed_ref[piece].astype(F32) for piece in range(4))
    bias = line_ref[192:193, :]
    for j in range(4):
        bias_ref[12 + j : 13 + j, :] = bias[:, 128 * j : 128 * j + 128]
    sublane = lax.broadcasted_iota(jnp.int32, (16, 128), 0)
    for piece in range(64):
        top, left = 12 * (piece // 4), 128 * (piece % 4)
        tile = jnp.where(sublane < 12, line_ref[top : top + 16, left : left + 128], bias_ref[...])
        out_ref[piece] = tile.astype(BF)


def tail_kernel(
    core_ref, rows_ref, local_ref, near_ref, next_ref, far_ref, last_ref, w_send_ref,
    upstream_ref, recv_ref, w_recv_ref, mesh_ref, grid_ref,
):
    product = lax.dot_general(
        recv_ref[...], w_recv_ref[...], (((1,), (1,)), ((), ())), preferred_element_type=F32
    )
    grid_ref[...] = (upstream_ref[...].astype(F32) + product).astype(BF)
    first_core = core_ref[0] == 0
    near, other = near_ref[...], next_ref[...]
    blocks = (
        jnp.where(first_core, near, other),
        jnp.where(first_core, other, near),
        far_ref[...],
        last_ref[...],
    )
    sublane = lax.broadcasted_iota(jnp.int32, (128, 16), 0)
    grad = local_ref[...]
    for j, block in enumerate(blocks):
        pick = (sublane == rows_ref[j : j + 1, :]).astype(F32).astype(BF)
        grad += jnp.dot(pick, block, preferred_element_type=F32)
    mesh_ref[...] = lax.dot_general(
        grad.astype(BF), w_send_ref[...], (((1,), (1,)), ((), ())), preferred_element_type=F32
    )


def shape(rows, dtype):
    return jax.ShapeDtypeStruct((rows, 512), dtype)


def edge_step(*args):
    return pl.pallas_call(
        edge_kernel,
        out_shape=(shape(800, BF), shape(192, BF), shape(192, BF), shape(512, BF), shape(512, BF), shape(128, F32))
        + (shape(16, BF),) * 3,
        in_specs=[SM] + [VM] * 5 + [HBM] * 7,
        out_specs=(VM,) * 9,
        scratch_shapes=[
            pltpu.VMEM((384, 512), BF),
            pltpu.VMEM((1536, 512), F32),
            pltpu.VMEM((1536, 512), BF),
            pltpu.VMEM((8, 512), F32),
            pltpu.VMEM((512, 512), BF),
            pltpu.VMEM((512, 512), F32),
            pltpu.VMEM((512, 512), F32),
            pltpu.SemaphoreType.DMA((7,)),
        ],
        compiler_params=limit(24),
        name="edge_step",
        cost_estimate=pl.CostEstimate(flops=3_000_000_000, bytes_accessed=6_000_000, transcendentals=800_000),
    )(*args)


def keep_step(*args):
    return pl.pallas_call(
        keep_kernel,
        out_shape=shape(768, F32),
        in_specs=[SM] + [VM] * 6,
        out_specs=VM,
        compiler_params=limit(10),
        name="keep_step",
        cost_estimate=pl.CostEstimate(flops=600_000_000, bytes_accessed=4_000_000, transcendentals=0),
    )(*args)


def pack_step(*args):
    return pl.pallas_call(
        pack_kernel,
        out_shape=(jax.ShapeDtypeStruct((4, 208, 512), BF), shape(16, BF)),
        in_specs=[VM] * 3,
        out_specs=(VM,) * 2,
        compiler_params=limit(8),
        name="pack_step",
        cost_estimate=pl.CostEstimate(flops=500_000, bytes_accessed=3_000_000, transcendentals=0),
    )(*args)


def pick_step(*args):
    return pl.pallas_call(
        pick_kernel,
        out_shape=(shape(16, BF),) * 4,
        in_specs=[HBM] * 2,
        out_specs=(VM,) * 4,
        scratch_shapes=[
            pltpu.VMEM((4, 16), jnp.int32),
            pltpu.VMEM((128, 512), BF),
            pltpu.SemaphoreType.DMA((2,)),
        ],
        name="pick_step",
        cost_estimate=pl.CostEstimate(flops=10_000_000, bytes_accessed=200_000, transcendentals=0),
    )(*args)


def line_step(packed):
    return pl.pallas_call(
        line_kernel,
        out_shape=jax.ShapeDtypeStruct((64, 16, 128), BF),
        in_specs=[HBM],
        out_specs=VM,
        scratch_shapes=[
            pltpu.VMEM((4, 208, 512), BF),
            pltpu.VMEM((208, 512), F32),
            pltpu.VMEM((16, 128), F32),
            pltpu.SemaphoreType.DMA((4,)),
        ],
        compiler_params=limit(8),
        name="line_step",
        cost_estimate=pl.CostEstimate(flops=500_000, bytes_accessed=1_000_000, transcendentals=0),
    )(packed)


def tail_step(*args):
    return pl.pallas_call(
        tail_kernel,
        out_shape=(shape(128, F32), shape(512, BF)),
        in_specs=[SM] + [VM] * 10,
        out_specs=(VM,) * 2,
        compiler_params=limit(8),
        name="tail_step",
        cost_estimate=pl.CostEstimate(flops=400_000_000, bytes_accessed=3_000_000, transcendentals=0),
    )(*args)


SPACE = ("y", "x", "core")
PLANE = ("dp", "y")


def shift_space(value, offset):
    pieces = lax.axis_size(SPACE)
    return lax.ppermute(value, SPACE, [(i, (i + offset) % pieces) for i in range(pieces)])


def swap_chips(value):
    pieces = lax.axis_size(SPACE)
    return lax.ppermute(
        value, SPACE, [(i, (i - 1 + 2 * (i % 2)) % pieces) for i in range(pieces)]
    )


def swap_cores(value):
    return lax.ppermute(value, "core", [(0, 1), (1, 0)])


def exchange(value, axes):
    return lax.all_to_all(value, axes, split_axis=0, concat_axis=0, tiled=True)


def gather_pieces(value, axes):
    spread = jnp.broadcast_to(value[None], (lax.axis_size(axes),) + value.shape)
    return exchange(spread, axes)


def per_device(
    mesh_latent, grid_latent, cotangent, sender_slot, send_rows, w_send, w_recv, w_node, edge_bias
):
    mesh_rows = mesh_latent[0]
    grid_rows = grid_latent[0]
    upstream = cotangent[0]
    core = lax.axis_index("core")
    core_ref = core.astype(jnp.int32).reshape(1)
    pieces = lax.axis_size(SPACE)
    offsets = (1, -1, max(2, pieces // 8), pieces // 2)
    outgoing = pick_step(send_rows[0], mesh_rows)
    halo = [shift_space(outgoing[j], offsets[j]) for j in range(4)]
    recv_proj = lax.dot_general(
        grid_rows, w_recv, (((1,), (0,)), ((), ())), preferred_element_type=F32
    ) + edge_bias
    agg_grad = lax.dot_general(
        upstream, w_node, (((1,), (1,)), ((), ())), preferred_element_type=F32
    )
    column = sender_slot.reshape(512, 3)
    row = column.T.reshape(1, 1536)
    send, known, slot, recv_grad, node, local, *leaving = edge_step(
        core_ref, column, row, mesh_rows, grid_rows, upstream, *halo, w_send, recv_proj, agg_grad
    )
    came = swap_cores(send)
    keep = keep_step(core_ref, known, slot, grid_rows, recv_grad, node, upstream)
    packed, near = pack_step(keep, came, send[768:784])
    packed, *early = lax.optimization_barrier((packed, *leaving[:2]))

    next_chip = swap_chips(early[0])
    far = shift_space(early[1], -offsets[2])
    line = line_step(exchange(packed, "x"))
    line, next_chip, far = lax.optimization_barrier((line, next_chip, far))

    factor = float(lax.axis_size("dp") * pieces * 512) ** (-0.5)
    total = jnp.sum(exchange(line, PLANE).astype(F32), axis=0) * factor
    total, *later = lax.optimization_barrier((total, *leaving[2:]))
    last = shift_space(later[0], -offsets[3])
    grad_bias = total[12:].reshape(512)
    plane = gather_pieces(total.astype(BF), PLANE)[:, :12].reshape(16, 4, 12, 128)
    plane = plane.transpose(0, 2, 1, 3).reshape(192, 512)
    grad_mesh, grad_grid = tail_step(
        core_ref, send_rows[0], local, near, next_chip, far, last, w_send, upstream, recv_grad, w_recv
    )
    plane, grad_mesh, grad_grid, grad_bias = lax.optimization_barrier(
        (plane, grad_mesh, grad_grid, grad_bias)
    )

    half = gather_pieces(plane, "x").reshape(3, 1, 256, 512)
    partner = swap_cores(half)
    low = jnp.where(core == 0, half, partner)
    high = jnp.where(core == 0, partner, half)
    whole = jnp.concatenate([low, high], axis=1).reshape(3, 512, 512)
    return (grad_mesh[None], grad_grid[None], whole[0], whole[1], whole[2], grad_bias)


def solution(mesh):
    fine = Mesh(mesh.devices.reshape(8, 8, 4, 2), ("dp",) + SPACE)
    placed = (
        P("dp", SPACE, None),
        P("dp", SPACE, None),
        P("dp", SPACE, None),
        P(SPACE),
        P(SPACE, None, None),
        P(),
        P(),
        P(),
        P(),
    )
    return jax.shard_map(
        per_device,
        mesh=fine,
        in_specs=placed,
        out_specs=(P("dp", SPACE, None), P("dp", SPACE, None), P(), P(), P(), P()),
        check_vma=False,
    )
```

```python
import jax
import jax.numpy as jnp
from jax import lax
from jax.experimental import pallas as pl
from jax.experimental.pallas import tpu as pltpu
from jax.sharding import Mesh, PartitionSpec as P

BF = jnp.bfloat16
F32 = jnp.float32


def rows_dot(left, right):
    return lax.dot_general(left, right, (((0,), (0,)), ((), ())), preferred_element_type=F32)


def half_terms(start, known_ref, slot_ref, grid_ref, recv_ref, node_ref, upstream_ref, out_ref):
    span = pl.ds(pl.multiple_of(start, 256), 256)
    pairs = ((known_ref, slot_ref), (grid_ref, recv_ref), (node_ref, upstream_ref))
    for index, (left_ref, right_ref) in enumerate(pairs):
        product = rows_dot(left_ref[:, span], right_ref[...])
        out_ref[index * 256 : (index + 1) * 256, :] = product.astype(out_ref.dtype)


def pick_kernel(rows_hbm, mesh_hbm, o0_ref, o1_ref, o2_ref, o3_ref, rows_ref, mesh_ref, arrived):
    mesh_copy = pltpu.make_async_copy(mesh_hbm, mesh_ref, arrived.at[0])
    rows_copy = pltpu.make_async_copy(rows_hbm, rows_ref, arrived.at[1])
    mesh_copy.start()
    rows_copy.start()
    rows_copy.wait()
    mesh_copy.wait()
    sublane = lax.broadcasted_iota(jnp.int32, (128, 16), 0)
    for j, out_ref in enumerate((o0_ref, o1_ref, o2_ref, o3_ref)):
        pick = (sublane == rows_ref[j : j + 1, :]).astype(F32).astype(BF)
        out_ref[...] = rows_dot(pick, mesh_ref[...]).astype(BF)


def edge_kernel(
    core_ref, column_ref, row_ref, mesh_ref, grid_ref, upstream_ref,
    h0_ref, h1_ref, h2_ref, h3_ref, w_hbm, recv_proj_hbm, agg_grad_hbm,
    send_ref, known_ref, slot_ref, recv_ref, node_ref, local_ref, next_ref, far_ref, last_ref,
    table_ref, preact_ref, edge_ref, bias_ref, w_send_ref, recv_proj_ref, agg_grad_ref, arrived,
):
    copies = [
        pltpu.make_async_copy(halo_ref, known_ref.at[pl.ds(128 + 16 * j, 16)], arrived.at[j])
        for j, halo_ref in enumerate((h0_ref, h1_ref, h2_ref, h3_ref))
    ]
    copies.append(pltpu.make_async_copy(w_hbm, w_send_ref, arrived.at[4]))
    copies.append(pltpu.make_async_copy(recv_proj_hbm, recv_proj_ref, arrived.at[5]))
    copies.append(pltpu.make_async_copy(agg_grad_hbm, agg_grad_ref, arrived.at[6]))
    for copy in copies:
        copy.start()
    known_ref[0:128, :] = mesh_ref[...]
    for copy in copies[:5]:
        copy.wait()
    sent = jnp.dot(known_ref[...], w_send_ref[...], preferred_element_type=F32)
    high = sent.astype(BF)
    table_ref[0:192, :] = high
    table_ref[192:384, :] = (sent - high.astype(F32)).astype(BF)
    lane = lax.broadcasted_iota(jnp.int32, (512, 384), 1)
    lane = jnp.where(lane >= 192, lane - 192, lane)
    for k in range(3):
        pick = (lane == column_ref[:, k : k + 1]).astype(F32).astype(BF)
        preact_ref[k * 512 : (k + 1) * 512, :] = jnp.dot(
            pick, table_ref[...], preferred_element_type=F32
        )
    copies[5].wait()
    copies[6].wait()
    bias_ref[...] = jnp.zeros_like(bias_ref)

    def chunk(step, carry):
        rows = pl.ds(pl.multiple_of(step * 16, 16), 16)
        recv_proj = recv_proj_ref[rows, :]
        agg_grad = agg_grad_ref[rows, :]
        node = jnp.zeros((16, 512), F32)
        recv = jnp.zeros((16, 512), F32)
        for k in range(3):
            edge_rows = pl.ds(pl.multiple_of(step * 16 + k * 512, 16), 16)
            preact = preact_ref[edge_rows, :] + recv_proj
            sigmoid = 0.5 * jnp.tanh(0.5 * preact) + 0.5
            silu = preact * sigmoid
            node += silu
            edge = (agg_grad * (sigmoid + silu * (1.0 - sigmoid))).astype(BF)
            edge_ref[edge_rows, :] = edge
            recv += edge.astype(F32)
        node_ref[rows, :] = node.astype(BF)
        recv_ref[rows, :] = recv.astype(BF)
        bias_ref[...] += recv[0:8] + recv[8:16]
        return carry

    lax.fori_loop(0, 32, chunk, 0)
    sublane = lax.broadcasted_iota(jnp.int32, (192, 1536), 0)
    spread = (sublane == row_ref[...]).astype(F32).astype(BF)
    slots = jnp.dot(spread, edge_ref[...], preferred_element_type=F32)
    local_ref[...] = slots[0:128]
    slot_ref[...] = slots.astype(BF)
    half_terms((1 - core_ref[0]) * 256, known_ref, slot_ref, grid_ref, recv_ref, node_ref, upstream_ref, send_ref)
    total = jnp.sum(bias_ref[...], axis=0, keepdims=True)
    send_ref[768:784, :] = jnp.broadcast_to(total, (16, 512)).astype(BF)
    leaving = pl.ds(pl.multiple_of(144 - 16 * core_ref[0], 16), 16)
    send_ref[784:800, :] = slot_ref[leaving, :]
    staying = pl.ds(pl.multiple_of(128 + 16 * core_ref[0], 16), 16)
    next_ref[...] = slot_ref[staying, :]
    far_ref[...] = slot_ref[160:176, :]
    last_ref[...] = slot_ref[176:192, :]


def keep_kernel(core_ref, known_ref, slot_ref, grid_ref, recv_ref, node_ref, upstream_ref, keep_ref):
    half_terms(core_ref[0] * 256, known_ref, slot_ref, grid_ref, recv_ref, node_ref, upstream_ref, keep_ref)


VM = pl.BlockSpec(memory_space=pltpu.VMEM)
HBM = pl.BlockSpec(memory_space=pltpu.HBM)
SM = pl.BlockSpec(memory_space=pltpu.SMEM)


def limit(mebibytes):
    return pltpu.CompilerParams(vmem_limit_bytes=mebibytes * 1024 * 1024)


def pack_kernel(keep_ref, came_ref, sent_ref, out_ref, near_ref):
    near_ref[...] = came_ref[784:800, :]
    bias = (sent_ref[...].astype(F32) + came_ref[768:784, :].astype(F32)).astype(BF)
    for piece in range(4):
        rows = slice(piece * 192, piece * 192 + 192)
        out_ref[piece, 0:192, :] = (keep_ref[rows, :] + came_ref[rows, :].astype(F32)).astype(BF)
        out_ref[piece, 192:208, :] = bias


def line_kernel(packed_hbm, out_ref, packed_ref, line_ref, bias_ref, arrived):
    copies = [
        pltpu.make_async_copy(packed_hbm.at[piece], packed_ref.at[piece], arrived.at[piece])
        for piece in range(4)
    ]
    for copy in copies:
        copy.start()
    for copy in copies:
        copy.wait()
    line_ref[...] = sum(packed_ref[piece].astype(F32) for piece in range(4))
    bias = line_ref[192:193, :]
    for j in range(4):
        bias_ref[12 + j : 13 + j, :] = bias[:, 128 * j : 128 * j + 128]
    sublane = lax.broadcasted_iota(jnp.int32, (16, 128), 0)
    for piece in range(64):
        top, left = 12 * (piece // 4), 128 * (piece % 4)
        tile = jnp.where(sublane < 12, line_ref[top : top + 16, left : left + 128], bias_ref[...])
        out_ref[piece] = tile.astype(BF)


def grid_kernel(upstream_ref, recv_ref, w_recv_ref, grid_ref):
    product = lax.dot_general(
        recv_ref[...], w_recv_ref[...], (((1,), (1,)), ((), ())), preferred_element_type=F32
    )
    grid_ref[...] = (upstream_ref[...].astype(F32) + product).astype(BF)


def mesh_kernel(
    core_ref, rows_ref, local_ref, near_ref, next_ref, far_ref, last_ref, w_send_ref, mesh_ref
):
    first_core = core_ref[0] == 0
    near, other = near_ref[...], next_ref[...]
    blocks = (
        jnp.where(first_core, near, other),
        jnp.where(first_core, other, near),
        far_ref[...],
        last_ref[...],
    )
    sublane = lax.broadcasted_iota(jnp.int32, (128, 16), 0)
    grad = local_ref[...]
    for j, block in enumerate(blocks):
        pick = (sublane == rows_ref[j : j + 1, :]).astype(F32).astype(BF)
        grad += jnp.dot(pick, block, preferred_element_type=F32)
    mesh_ref[...] = lax.dot_general(
        grad.astype(BF), w_send_ref[...], (((1,), (1,)), ((), ())), preferred_element_type=F32
    )


def shape(rows, dtype):
    return jax.ShapeDtypeStruct((rows, 512), dtype)


def edge_step(*args):
    return pl.pallas_call(
        edge_kernel,
        out_shape=(shape(800, BF), shape(192, BF), shape(192, BF), shape(512, BF), shape(512, BF), shape(128, F32))
        + (shape(16, BF),) * 3,
        in_specs=[SM] + [VM] * 5 + [HBM] * 7,
        out_specs=(VM,) * 9,
        scratch_shapes=[
            pltpu.VMEM((384, 512), BF),
            pltpu.VMEM((1536, 512), F32),
            pltpu.VMEM((1536, 512), BF),
            pltpu.VMEM((8, 512), F32),
            pltpu.VMEM((512, 512), BF),
            pltpu.VMEM((512, 512), F32),
            pltpu.VMEM((512, 512), F32),
            pltpu.SemaphoreType.DMA((7,)),
        ],
        compiler_params=limit(24),
        name="edge_step",
        cost_estimate=pl.CostEstimate(flops=3_000_000_000, bytes_accessed=6_000_000, transcendentals=800_000),
    )(*args)


def keep_step(*args):
    return pl.pallas_call(
        keep_kernel,
        out_shape=shape(768, F32),
        in_specs=[SM] + [VM] * 6,
        out_specs=VM,
        compiler_params=limit(10),
        name="keep_step",
        cost_estimate=pl.CostEstimate(flops=600_000_000, bytes_accessed=4_000_000, transcendentals=0),
    )(*args)


def pack_step(*args):
    return pl.pallas_call(
        pack_kernel,
        out_shape=(jax.ShapeDtypeStruct((4, 208, 512), BF), shape(16, BF)),
        in_specs=[VM] * 3,
        out_specs=(VM,) * 2,
        compiler_params=limit(8),
        name="pack_step",
        cost_estimate=pl.CostEstimate(flops=500_000, bytes_accessed=3_000_000, transcendentals=0),
    )(*args)


def pick_step(*args):
    return pl.pallas_call(
        pick_kernel,
        out_shape=(shape(16, BF),) * 4,
        in_specs=[HBM] * 2,
        out_specs=(VM,) * 4,
        scratch_shapes=[
            pltpu.VMEM((4, 16), jnp.int32),
            pltpu.VMEM((128, 512), BF),
            pltpu.SemaphoreType.DMA((2,)),
        ],
        name="pick_step",
        cost_estimate=pl.CostEstimate(flops=10_000_000, bytes_accessed=200_000, transcendentals=0),
    )(*args)


def line_step(packed):
    return pl.pallas_call(
        line_kernel,
        out_shape=jax.ShapeDtypeStruct((64, 16, 128), BF),
        in_specs=[HBM],
        out_specs=VM,
        scratch_shapes=[
            pltpu.VMEM((4, 208, 512), BF),
            pltpu.VMEM((208, 512), F32),
            pltpu.VMEM((16, 128), F32),
            pltpu.SemaphoreType.DMA((4,)),
        ],
        compiler_params=limit(8),
        name="line_step",
        cost_estimate=pl.CostEstimate(flops=500_000, bytes_accessed=1_000_000, transcendentals=0),
    )(packed)


def grid_step(*args):
    return pl.pallas_call(
        grid_kernel,
        out_shape=shape(512, BF),
        in_specs=[VM] * 3,
        out_specs=VM,
        compiler_params=limit(6),
        name="grid_step",
        cost_estimate=pl.CostEstimate(flops=300_000_000, bytes_accessed=2_000_000, transcendentals=0),
    )(*args)


def mesh_step(*args):
    return pl.pallas_call(
        mesh_kernel,
        out_shape=shape(128, F32),
        in_specs=[SM] + [VM] * 7,
        out_specs=VM,
        compiler_params=limit(6),
        name="mesh_step",
        cost_estimate=pl.CostEstimate(flops=80_000_000, bytes_accessed=1_000_000, transcendentals=0),
    )(*args)


SPACE = ("y", "x", "core")
PLANE = ("dp", "y")


def shift_space(value, offset):
    pieces = lax.axis_size(SPACE)
    return lax.ppermute(value, SPACE, [(i, (i + offset) % pieces) for i in range(pieces)])


def swap_chips(value):
    pieces = lax.axis_size(SPACE)
    return lax.ppermute(
        value, SPACE, [(i, (i - 1 + 2 * (i % 2)) % pieces) for i in range(pieces)]
    )


def swap_cores(value):
    return lax.ppermute(value, "core", [(0, 1), (1, 0)])


def exchange(value, axes):
    return lax.all_to_all(value, axes, split_axis=0, concat_axis=0, tiled=True)


def gather_pieces(value, axes):
    spread = jnp.broadcast_to(value[None], (lax.axis_size(axes),) + value.shape)
    return exchange(spread, axes)


def per_device(
    mesh_latent, grid_latent, cotangent, sender_slot, send_rows, w_send, w_recv, w_node, edge_bias
):
    mesh_rows = mesh_latent[0]
    grid_rows = grid_latent[0]
    upstream = cotangent[0]
    core = lax.axis_index("core")
    core_ref = core.astype(jnp.int32).reshape(1)
    pieces = lax.axis_size(SPACE)
    offsets = (1, -1, max(2, pieces // 8), pieces // 2)
    outgoing = pick_step(send_rows[0], mesh_rows)
    halo = [shift_space(outgoing[j], offsets[j]) for j in range(4)]
    recv_proj = lax.dot_general(
        grid_rows, w_recv, (((1,), (0,)), ((), ())), preferred_element_type=F32
    ) + edge_bias
    agg_grad = lax.dot_general(
        upstream, w_node, (((1,), (1,)), ((), ())), preferred_element_type=F32
    )
    column = sender_slot.reshape(512, 3)
    row = column.T.reshape(1, 1536)
    send, known, slot, recv_grad, node, local, *leaving = edge_step(
        core_ref, column, row, mesh_rows, grid_rows, upstream, *halo, w_send, recv_proj, agg_grad
    )
    came = swap_cores(send)
    keep = keep_step(core_ref, known, slot, grid_rows, recv_grad, node, upstream)
    packed, near = pack_step(keep, came, send[768:784])
    packed, *early = lax.optimization_barrier((packed, *leaving[:2]))

    next_chip = swap_chips(early[0])
    far = shift_space(early[1], -offsets[2])
    line = line_step(exchange(packed, "x"))
    grad_grid = grid_step(upstream, recv_grad, w_recv)
    line, next_chip, far, grad_grid = lax.optimization_barrier((line, next_chip, far, grad_grid))

    factor = float(lax.axis_size("dp") * pieces * 512) ** (-0.5)
    total = jnp.sum(exchange(line, PLANE).astype(F32), axis=0) * factor
    total, *later = lax.optimization_barrier((total, *leaving[2:]))
    last = shift_space(later[0], -offsets[3])
    grad_bias = total[12:].reshape(512)
    plane = gather_pieces(total.astype(BF), PLANE)[:, :12].reshape(16, 4, 12, 128)
    plane = plane.transpose(0, 2, 1, 3).reshape(192, 512)
    plane, last, grad_bias = lax.optimization_barrier((plane, last, grad_bias))

    half = gather_pieces(plane, "x").reshape(3, 1, 256, 512)
    partner = swap_cores(half)
    grad_mesh = mesh_step(core_ref, send_rows[0], local, near, next_chip, far, last, w_send)
    low = jnp.where(core == 0, half, partner)
    high = jnp.where(core == 0, partner, half)
    whole = jnp.concatenate([low, high], axis=1).reshape(3, 512, 512)
    return (grad_mesh[None], grad_grid[None], whole[0], whole[1], whole[2], grad_bias)


def solution(mesh):
    fine = Mesh(mesh.devices.reshape(8, 8, 4, 2), ("dp",) + SPACE)
    placed = (
        P("dp", SPACE, None),
        P("dp", SPACE, None),
        P("dp", SPACE, None),
        P(SPACE),
        P(SPACE, None, None),
        P(),
        P(),
        P(),
        P(),
    )
    return jax.shard_map(
        per_device,
        mesh=fine,
        in_specs=placed,
        out_specs=(P("dp", SPACE, None), P("dp", SPACE, None), P(), P(), P(), P()),
        check_vma=False,
    )
```

```python
import jax
import jax.numpy as jnp
from jax import lax
from jax.experimental import pallas as pl
from jax.experimental.pallas import tpu as pltpu
from jax.sharding import Mesh, PartitionSpec as P

BF = jnp.bfloat16
F32 = jnp.float32


def rows_dot(left, right):
    return lax.dot_general(left, right, (((0,), (0,)), ((), ())), preferred_element_type=F32)


def half_terms(start, known_ref, slot_ref, grid_ref, recv_ref, node_ref, upstream_ref, out_ref):
    span = pl.ds(pl.multiple_of(start, 256), 256)
    pairs = ((known_ref, slot_ref), (grid_ref, recv_ref), (node_ref, upstream_ref))
    for index, (left_ref, right_ref) in enumerate(pairs):
        product = rows_dot(left_ref[:, span], right_ref[...])
        out_ref[index * 256 : (index + 1) * 256, :] = product.astype(out_ref.dtype)


def pick_kernel(core_ref, rows_hbm, mesh_hbm, o0_ref, o1_ref, o2_ref, o3_ref, rows_ref, mesh_ref, arrived):
    mesh_copy = pltpu.make_async_copy(mesh_hbm, mesh_ref, arrived.at[0])
    rows_copy = pltpu.make_async_copy(rows_hbm, rows_ref, arrived.at[1])
    mesh_copy.start()
    rows_copy.start()
    rows_copy.wait()
    mesh_copy.wait()
    sublane = lax.broadcasted_iota(jnp.int32, (128, 16), 0)
    blocks = (core_ref[0], 1 - core_ref[0], 2, 3)
    for j, out_ref in zip(blocks, (o0_ref, o1_ref, o2_ref, o3_ref)):
        pick = (sublane == rows_ref[pl.ds(j, 1), :]).astype(F32).astype(BF)
        out_ref[...] = rows_dot(pick, mesh_ref[...]).astype(BF)


def edge_kernel(
    core_ref, column_ref, row_ref, mesh_ref, grid_ref, upstream_ref,
    h0_ref, h1_ref, h2_ref, h3_ref, w_hbm, recv_proj_hbm, agg_grad_hbm,
    send_ref, known_ref, slot_ref, recv_ref, node_ref, local_ref, next_ref, far_ref, last_ref,
    table_ref, preact_ref, edge_ref, bias_ref, w_send_ref, recv_proj_ref, agg_grad_ref, halo_rows_ref, arrived,
):
    copies = [
        pltpu.make_async_copy(halo_ref, halo_rows_ref.at[pl.ds(16 * j, 16)], arrived.at[j])
        for j, halo_ref in enumerate((h0_ref, h1_ref, h2_ref, h3_ref))
    ]
    copies.append(pltpu.make_async_copy(w_hbm, w_send_ref, arrived.at[4]))
    copies.append(pltpu.make_async_copy(recv_proj_hbm, recv_proj_ref, arrived.at[5]))
    copies.append(pltpu.make_async_copy(agg_grad_hbm, agg_grad_ref, arrived.at[6]))
    for copy in copies:
        copy.start()
    known_ref[0:128, :] = mesh_ref[...]
    for copy in copies[:5]:
        copy.wait()
    partner = pl.ds(pl.multiple_of(144 - 16 * core_ref[0], 16), 16)
    next_chip = pl.ds(pl.multiple_of(128 + 16 * core_ref[0], 16), 16)
    known_ref[partner, :] = halo_rows_ref[0:16, :]
    known_ref[next_chip, :] = halo_rows_ref[16:32, :]
    known_ref[160:192, :] = halo_rows_ref[32:64, :]
    sent = jnp.dot(known_ref[...], w_send_ref[...], preferred_element_type=F32)
    high = sent.astype(BF)
    table_ref[0:192, :] = high
    table_ref[192:384, :] = (sent - high.astype(F32)).astype(BF)
    lane = lax.broadcasted_iota(jnp.int32, (512, 384), 1)
    lane = jnp.where(lane >= 192, lane - 192, lane)
    for k in range(3):
        pick = (lane == column_ref[:, k : k + 1]).astype(F32).astype(BF)
        preact_ref[k * 512 : (k + 1) * 512, :] = jnp.dot(
            pick, table_ref[...], preferred_element_type=F32
        )
    copies[5].wait()
    copies[6].wait()
    bias_ref[...] = jnp.zeros_like(bias_ref)

    def chunk(step, carry):
        rows = pl.ds(pl.multiple_of(step * 16, 16), 16)
        recv_proj = recv_proj_ref[rows, :]
        agg_grad = agg_grad_ref[rows, :]
        node = jnp.zeros((16, 512), F32)
        recv = jnp.zeros((16, 512), F32)
        for k in range(3):
            edge_rows = pl.ds(pl.multiple_of(step * 16 + k * 512, 16), 16)
            preact = preact_ref[edge_rows, :] + recv_proj
            sigmoid = 0.5 * jnp.tanh(0.5 * preact) + 0.5
            silu = preact * sigmoid
            node += silu
            edge = (agg_grad * (sigmoid + silu * (1.0 - sigmoid))).astype(BF)
            edge_ref[edge_rows, :] = edge
            recv += edge.astype(F32)
        node_ref[rows, :] = node.astype(BF)
        recv_ref[rows, :] = recv.astype(BF)
        bias_ref[...] += recv[0:8] + recv[8:16]
        return carry

    lax.fori_loop(0, 32, chunk, 0)
    sublane = lax.broadcasted_iota(jnp.int32, (192, 1536), 0)
    spread = (sublane == row_ref[...]).astype(F32).astype(BF)
    slots = jnp.dot(spread, edge_ref[...], preferred_element_type=F32)
    local_ref[...] = slots[0:128]
    slot_ref[...] = slots.astype(BF)
    half_terms((1 - core_ref[0]) * 256, known_ref, slot_ref, grid_ref, recv_ref, node_ref, upstream_ref, send_ref)
    total = jnp.sum(bias_ref[...], axis=0, keepdims=True)
    send_ref[768:784, :] = jnp.broadcast_to(total, (16, 512)).astype(BF)
    leaving = pl.ds(pl.multiple_of(144 - 16 * core_ref[0], 16), 16)
    send_ref[784:800, :] = slot_ref[leaving, :]
    staying = pl.ds(pl.multiple_of(128 + 16 * core_ref[0], 16), 16)
    next_ref[...] = slot_ref[staying, :]
    far_ref[...] = slot_ref[160:176, :]
    last_ref[...] = slot_ref[176:192, :]


def keep_kernel(core_ref, known_ref, slot_ref, grid_ref, recv_ref, node_ref, upstream_ref, keep_ref):
    half_terms(core_ref[0] * 256, known_ref, slot_ref, grid_ref, recv_ref, node_ref, upstream_ref, keep_ref)


VM = pl.BlockSpec(memory_space=pltpu.VMEM)
HBM = pl.BlockSpec(memory_space=pltpu.HBM)
SM = pl.BlockSpec(memory_space=pltpu.SMEM)


def limit(mebibytes):
    return pltpu.CompilerParams(vmem_limit_bytes=mebibytes * 1024 * 1024)


def pack_kernel(keep_ref, came_ref, sent_ref, out_ref, near_ref):
    near_ref[...] = came_ref[784:800, :]
    bias = (sent_ref[...].astype(F32) + came_ref[768:784, :].astype(F32)).astype(BF)
    for piece in range(4):
        rows = slice(piece * 192, piece * 192 + 192)
        out_ref[piece, 0:192, :] = (keep_ref[rows, :] + came_ref[rows, :].astype(F32)).astype(BF)
        out_ref[piece, 192:208, :] = bias


def line_kernel(packed_hbm, out_ref, packed_ref, line_ref, bias_ref, arrived):
    copies = [
        pltpu.make_async_copy(packed_hbm.at[piece], packed_ref.at[piece], arrived.at[piece])
        for piece in range(4)
    ]
    for copy in copies:
        copy.start()
    for copy in copies:
        copy.wait()
    line_ref[...] = sum(packed_ref[piece].astype(F32) for piece in range(4))
    bias = line_ref[192:193, :]
    for j in range(4):
        bias_ref[12 + j : 13 + j, :] = bias[:, 128 * j : 128 * j + 128]
    sublane = lax.broadcasted_iota(jnp.int32, (16, 128), 0)
    for piece in range(64):
        top, left = 12 * (piece // 4), 128 * (piece % 4)
        tile = jnp.where(sublane < 12, line_ref[top : top + 16, left : left + 128], bias_ref[...])
        out_ref[piece] = tile.astype(BF)


def tail_kernel(
    core_ref, rows_ref, local_ref, near_ref, next_ref, far_ref, last_ref, w_send_ref,
    upstream_ref, recv_ref, w_recv_ref, mesh_ref, grid_ref,
):
    product = lax.dot_general(
        recv_ref[...], w_recv_ref[...], (((1,), (1,)), ((), ())), preferred_element_type=F32
    )
    grid_ref[...] = (upstream_ref[...].astype(F32) + product).astype(BF)
    first_core = core_ref[0] == 0
    near, other = near_ref[...], next_ref[...]
    blocks = (
        jnp.where(first_core, near, other),
        jnp.where(first_core, other, near),
        far_ref[...],
        last_ref[...],
    )
    sublane = lax.broadcasted_iota(jnp.int32, (128, 16), 0)
    grad = local_ref[...]
    for j, block in enumerate(blocks):
        pick = (sublane == rows_ref[j : j + 1, :]).astype(F32).astype(BF)
        grad += jnp.dot(pick, block, preferred_element_type=F32)
    mesh_ref[...] = lax.dot_general(
        grad.astype(BF), w_send_ref[...], (((1,), (1,)), ((), ())), preferred_element_type=F32
    )


def shape(rows, dtype):
    return jax.ShapeDtypeStruct((rows, 512), dtype)


def edge_step(*args):
    return pl.pallas_call(
        edge_kernel,
        out_shape=(shape(800, BF), shape(192, BF), shape(192, BF), shape(512, BF), shape(512, BF), shape(128, F32))
        + (shape(16, BF),) * 3,
        in_specs=[SM] + [VM] * 5 + [HBM] * 7,
        out_specs=(VM,) * 9,
        scratch_shapes=[
            pltpu.VMEM((384, 512), BF),
            pltpu.VMEM((1536, 512), F32),
            pltpu.VMEM((1536, 512), BF),
            pltpu.VMEM((8, 512), F32),
            pltpu.VMEM((512, 512), BF),
            pltpu.VMEM((512, 512), F32),
            pltpu.VMEM((512, 512), F32),
            pltpu.VMEM((64, 512), BF),
            pltpu.SemaphoreType.DMA((7,)),
        ],
        compiler_params=limit(24),
        name="edge_step",
        cost_estimate=pl.CostEstimate(flops=3_000_000_000, bytes_accessed=6_000_000, transcendentals=800_000),
    )(*args)


def keep_step(*args):
    return pl.pallas_call(
        keep_kernel,
        out_shape=shape(768, F32),
        in_specs=[SM] + [VM] * 6,
        out_specs=VM,
        compiler_params=limit(10),
        name="keep_step",
        cost_estimate=pl.CostEstimate(flops=600_000_000, bytes_accessed=4_000_000, transcendentals=0),
    )(*args)


def pack_step(*args):
    return pl.pallas_call(
        pack_kernel,
        out_shape=(jax.ShapeDtypeStruct((4, 208, 512), BF), shape(16, BF)),
        in_specs=[VM] * 3,
        out_specs=(VM,) * 2,
        compiler_params=limit(8),
        name="pack_step",
        cost_estimate=pl.CostEstimate(flops=500_000, bytes_accessed=3_000_000, transcendentals=0),
    )(*args)


def pick_step(*args):
    return pl.pallas_call(
        pick_kernel,
        out_shape=(shape(16, BF),) * 4,
        in_specs=[SM] + [HBM] * 2,
        out_specs=(VM,) * 4,
        scratch_shapes=[
            pltpu.VMEM((4, 16), jnp.int32),
            pltpu.VMEM((128, 512), BF),
            pltpu.SemaphoreType.DMA((2,)),
        ],
        name="pick_step",
        cost_estimate=pl.CostEstimate(flops=10_000_000, bytes_accessed=200_000, transcendentals=0),
    )(*args)


def line_step(packed):
    return pl.pallas_call(
        line_kernel,
        out_shape=jax.ShapeDtypeStruct((64, 16, 128), BF),
        in_specs=[HBM],
        out_specs=VM,
        scratch_shapes=[
            pltpu.VMEM((4, 208, 512), BF),
            pltpu.VMEM((208, 512), F32),
            pltpu.VMEM((16, 128), F32),
            pltpu.SemaphoreType.DMA((4,)),
        ],
        compiler_params=limit(8),
        name="line_step",
        cost_estimate=pl.CostEstimate(flops=500_000, bytes_accessed=1_000_000, transcendentals=0),
    )(packed)


def tail_step(*args):
    return pl.pallas_call(
        tail_kernel,
        out_shape=(shape(128, F32), shape(512, BF)),
        in_specs=[SM] + [VM] * 10,
        out_specs=(VM,) * 2,
        compiler_params=limit(8),
        name="tail_step",
        cost_estimate=pl.CostEstimate(flops=400_000_000, bytes_accessed=3_000_000, transcendentals=0),
    )(*args)


SPACE = ("y", "x", "core")
PLANE = ("dp", "y")


def shift_space(value, offset):
    pieces = lax.axis_size(SPACE)
    return lax.ppermute(value, SPACE, [(i, (i + offset) % pieces) for i in range(pieces)])


def swap_chips(value):
    pieces = lax.axis_size(SPACE)
    return lax.ppermute(
        value, SPACE, [(i, (i - 1 + 2 * (i % 2)) % pieces) for i in range(pieces)]
    )


def swap_cores(value):
    return lax.ppermute(value, "core", [(0, 1), (1, 0)])


def exchange(value, axes):
    return lax.all_to_all(value, axes, split_axis=0, concat_axis=0, tiled=True)


def gather_pieces(value, axes):
    spread = jnp.broadcast_to(value[None], (lax.axis_size(axes),) + value.shape)
    return exchange(spread, axes)


def per_device(
    mesh_latent, grid_latent, cotangent, sender_slot, send_rows, w_send, w_recv, w_node, edge_bias
):
    mesh_rows = mesh_latent[0]
    grid_rows = grid_latent[0]
    upstream = cotangent[0]
    core = lax.axis_index("core")
    core_ref = core.astype(jnp.int32).reshape(1)
    pieces = lax.axis_size(SPACE)
    offsets = (1, -1, max(2, pieces // 8), pieces // 2)
    outgoing = pick_step(core_ref, send_rows[0], mesh_rows)
    halo = [swap_cores(outgoing[0]), swap_chips(outgoing[1])]
    halo += [shift_space(outgoing[j], offsets[j]) for j in (2, 3)]
    recv_proj = lax.dot_general(
        grid_rows, w_recv, (((1,), (0,)), ((), ())), preferred_element_type=F32
    ) + edge_bias
    agg_grad = lax.dot_general(
        upstream, w_node, (((1,), (1,)), ((), ())), preferred_element_type=F32
    )
    column = sender_slot.reshape(512, 3)
    row = column.T.reshape(1, 1536)
    send, known, slot, recv_grad, node, local, *leaving = edge_step(
        core_ref, column, row, mesh_rows, grid_rows, upstream, *halo, w_send, recv_proj, agg_grad
    )
    came = swap_cores(send)
    keep = keep_step(core_ref, known, slot, grid_rows, recv_grad, node, upstream)
    packed, near = pack_step(keep, came, send[768:784])
    packed, *early = lax.optimization_barrier((packed, *leaving[:2]))

    next_chip = swap_chips(early[0])
    far = shift_space(early[1], -offsets[2])
    line = line_step(exchange(packed, "x"))
    line, next_chip, far = lax.optimization_barrier((line, next_chip, far))

    factor = float(lax.axis_size("dp") * pieces * 512) ** (-0.5)
    total = jnp.sum(exchange(line, PLANE).astype(F32), axis=0) * factor
    total, *later = lax.optimization_barrier((total, *leaving[2:]))
    last = shift_space(later[0], -offsets[3])
    grad_bias = total[12:].reshape(512)
    plane = gather_pieces(total.astype(BF), PLANE)[:, :12].reshape(16, 4, 12, 128)
    plane = plane.transpose(0, 2, 1, 3).reshape(192, 512)
    grad_mesh, grad_grid = tail_step(
        core_ref, send_rows[0], local, near, next_chip, far, last, w_send, upstream, recv_grad, w_recv
    )
    plane, grad_mesh, grad_grid, grad_bias = lax.optimization_barrier(
        (plane, grad_mesh, grad_grid, grad_bias)
    )

    half = gather_pieces(plane, "x").reshape(3, 1, 256, 512)
    partner = swap_cores(half)
    low = jnp.where(core == 0, half, partner)
    high = jnp.where(core == 0, partner, half)
    whole = jnp.concatenate([low, high], axis=1).reshape(3, 512, 512)
    return (grad_mesh[None], grad_grid[None], whole[0], whole[1], whole[2], grad_bias)


def solution(mesh):
    fine = Mesh(mesh.devices.reshape(8, 8, 4, 2), ("dp",) + SPACE)
    placed = (
        P("dp", SPACE, None),
        P("dp", SPACE, None),
        P("dp", SPACE, None),
        P(SPACE),
        P(SPACE, None, None),
        P(),
        P(),
        P(),
        P(),
    )
    return jax.shard_map(
        per_device,
        mesh=fine,
        in_specs=placed,
        out_specs=(P("dp", SPACE, None), P("dp", SPACE, None), P(), P(), P(), P()),
        check_vma=False,
    )
```
